768 devices in a mesh: dp: 256 (over x, z_hi, y, core), mp: 3 (over z_lo).
Axes of the slice: x: 4, y: 8, z: 12 (z_hi: 4, z_lo: 3; z = z_hi * 3 + z_lo), core: 2. Of those that a mesh axis runs over, the one named last changes fastest.
Arguments:
- picture_embedding_matrix: bfloat16 [147456, 1152], P(('dp', 'mp')), may hold values from -0.1875 to 0.1875
- caption_embedding_matrix: bfloat16 [147456, 1152], P(('dp', 'mp')), may hold values from -0.1875 to 0.1875
- positive_caption_indices: int32 [147456], P(('dp', 'mp')), may hold values from 0 to 147455, as said below
- sharpness_multiplier: float32 [1], replicated, may hold values from 5 to 15
- additive_shift_term: float32 [1], replicated, may hold values from -3 to -1
Outputs:
- grad_image: float32 [147456, 1152], P(('dp', 'mp'))
- grad_text: float32 [147456, 1152], P(('dp', 'mp'))
The draws below stay inside these ranges and needn't reach their ends.
Inputs may be any that keep to these rules, and one draw needn't show every extreme that they name: positive_caption_indices[i] names a text of row i's own block of 192 rows, and each text of a block is named once.
All inputs are finite; a program needn't handle non-finite values.
Results may differ from the reference program's by a relative error of at most 0.0027.
Values may be sent and summed in bfloat16 or wider, within the bound.
No kernel may reach another device: no remote copies, remote signals or barrier semaphores. Data moves between devices by JAX's collectives and lax.ppermute only.
A program may use at most 32 MiB of HBM per device.

```python
import jax
import jax.numpy as jnp
from jax import lax

D = 1152
TOK_DEV = 192
STEPS = 8
TOKENS = 147456


def draw_positive_caption_indices(key, part):
    key = jax.random.fold_in(key, 7)
    nblocks = TOKENS // TOK_DEV
    keys = jax.random.split(key, nblocks)
    perms = jax.vmap(lambda sub: jax.random.permutation(sub, TOK_DEV))(keys)
    base = jnp.arange(nblocks, dtype=jnp.int32)[:, None] * TOK_DEV
    return (perms.astype(jnp.int32) + base).reshape(TOKENS)


def levels(own_key, extent, pieces, smallest, largest):
    def one(position, parts):
        steps = jax.random.uniform(jax.random.fold_in(jax.random.fold_in(own_key, 6), position), (parts,), jnp.float32, smallest / len(pieces), largest / len(pieces))
        return jnp.repeat(jnp.exp(steps), extent[position] // parts).reshape((-1,) + (1,) * (len(extent) - position - 1))

    gain = one(*pieces[0])
    for cut in pieces[1:]:
        gain = gain * one(*cut)
    return gain


def scatter_about(key, dims, scale, reach, cuts=(), kind=jnp.bfloat16):
    array = scale * jax.random.normal(key, dims, jnp.float32)
    if cuts:
        array = array * levels(key, dims, cuts, -0.22, 0.18)
    return jnp.clip(array, -reach, reach).astype(kind)


def setup_inputs(seed: int = 0) -> dict:
    key_of = jax.random.split(jax.random.key(seed), 6)
    return {
        "picture_embedding_matrix": scatter_about(key_of[0], (TOKENS, D), D ** -0.5, 0.1875, ((0, 768),)),
        "caption_embedding_matrix": scatter_about(key_of[1], (TOKENS, D), D ** -0.5, 0.1875, ((0, 768),)),
        "positive_caption_indices": draw_positive_caption_indices(jax.random.fold_in(key_of[5], 71), 0),
        "sharpness_multiplier": jnp.clip(jax.random.uniform(key_of[3], (1,), jnp.float32, 5.0, 15.0), 5.0, 15.0),
        "additive_shift_term": jnp.clip(jax.random.uniform(key_of[4], (1,), jnp.float32, -3.0, -1.0), -3.0, -1.0),
    }


def objective_weighting_coefficients(picture_sample_count, caption_sample_count, desired_match_indicator, segment_start_position, sharpness_multiplier, additive_shift_term):
    couple_similarity_scores = lax.dot_general(picture_sample_count, caption_sample_count, (((1,), (1,)), ((), ())), preferred_element_type=jnp.float32)
    tempered_similarity_scores = sharpness_multiplier[0] * couple_similarity_scores + additive_shift_term[0]
    columns = segment_start_position + jnp.arange(caption_sample_count.shape[0], dtype=jnp.int32)
    match_polarity = jnp.where(desired_match_indicator[:, None] == columns[None, :], 1.0, -1.0).astype(jnp.float32)
    couple_coefficient = sharpness_multiplier[0] * (-match_polarity) * jax.nn.sigmoid(-match_polarity * tempered_similarity_scores)
    return couple_coefficient.astype(jnp.bfloat16)


def reference(picture_embedding_matrix, caption_embedding_matrix, positive_caption_indices, sharpness_multiplier, additive_shift_term):
    nblocks = TOKENS // TOK_DEV

    def block_step(grad_text, block):
        first = (block * TOK_DEV).astype(jnp.int32)
        picture_sample_count = lax.dynamic_slice_in_dim(picture_embedding_matrix, first, TOK_DEV, 0)
        desired_match_indicator = lax.dynamic_slice_in_dim(positive_caption_indices, first, TOK_DEV, 0)
        grad_rows = jnp.zeros((TOK_DEV, D), jnp.float32)
        for step in range(STEPS):
            other = (block - step) % nblocks
            segment_start_position = (other * TOK_DEV).astype(jnp.int32)
            caption_sample_count = lax.dynamic_slice_in_dim(caption_embedding_matrix, segment_start_position, TOK_DEV, 0)
            couple_coefficient = objective_weighting_coefficients(picture_sample_count, caption_sample_count, desired_match_indicator, segment_start_position, sharpness_multiplier, additive_shift_term)
            grad_rows = grad_rows + jnp.dot(couple_coefficient, caption_sample_count, preferred_element_type=jnp.float32)
            share = lax.dot_general(couple_coefficient, picture_sample_count, (((0,), (0,)), ((), ())), preferred_element_type=jnp.float32)
            current = lax.dynamic_slice_in_dim(grad_text, segment_start_position, TOK_DEV, 0)
            grad_text = lax.dynamic_update_slice_in_dim(grad_text, current + share, segment_start_position, 0)
        return grad_text, grad_rows

    grad_text, grad_blocks = lax.scan(block_step, jnp.zeros((TOKENS, D), jnp.float32), jnp.arange(nblocks, dtype=jnp.int32))
    return grad_blocks.reshape(TOKENS, D), grad_text
```

```python
import jax
import jax.numpy as jnp
from jax import lax
from jax.sharding import PartitionSpec as P

AXES = ("dp", "mp")
ROWS = 192
LINE = 3
GROUP = 6
LAP = 8
NB = 768
LOW = jnp.bfloat16


def lap_of(b):
    return (b // GROUP) % LAP


def sent(value, target):
    pairs = [(b, target(b) % NB) for b in range(NB) if target(b) is not None]
    return lax.ppermute(value, AXES, pairs)


def line_turned(value, by):
    return sent(value, lambda b: b // LINE * LINE + (b + by) % LINE)


def group_onward(value, y):
    half = ROWS // 2
    main = sent(value, lambda b: b + GROUP if lap_of(b) < LAP - 1 else b - GROUP * (LAP - 1))
    direct = sent(value[half:], lambda b: b + GROUP if lap_of(b) == LAP - 1 else None)
    relayed = sent(main[:half], lambda b: b + GROUP * LAP if lap_of(b) == 0 else None)
    return jnp.where(y == 0, jnp.concatenate([relayed, direct]), main)


def group_back(value, y):
    half = ROWS // 2
    main = sent(value, lambda b: b - GROUP if lap_of(b) > 0 else b + GROUP * (LAP - 1))
    direct = sent(value[half:], lambda b: b - GROUP if lap_of(b) == 0 else None)
    relayed = sent(main[:half], lambda b: b - GROUP * LAP if lap_of(b) == LAP - 1 else None)
    return jnp.where(y == LAP - 1, jnp.concatenate([relayed, direct]), main)


def on_device(
    picture_embedding_matrix,
    caption_embedding_matrix,
    positive_caption_indices,
    sharpness_multiplier,
    additive_shift_term,
):
    here = lax.axis_index(AXES)
    k = here % LINE
    core = here // LINE % 2
    y = lap_of(here)
    scale = sharpness_multiplier[0]
    shift = additive_shift_term[0]
    images = [picture_embedding_matrix]
    text0 = caption_embedding_matrix
    text2 = group_onward(text0, y)
    images += [line_turned(picture_embedding_matrix, r) for r in (1, 2)]
    far = sent(text0, lambda b: b + 3 * LINE if b % GROUP == 5 else None)
    near = sent(text0, lambda b: b + LINE if b // LINE % 2 == 0 else None)
    crossed = sent(text2, lambda b: b + LINE if b // LINE % 2 == 0 else b - LINE)
    text1 = jnp.where(core == 1, near, crossed)
    text3 = jnp.where(core == 1, crossed, far)

    def negatives(logits):
        return scale * jax.nn.sigmoid(scale * logits + shift)

    def scores(a, b):
        return lax.dot_general(a, b, (((1,), (1,)), ((), ())), preferred_element_type=jnp.float32)

    def over_texts(coef, texts):
        return jnp.dot(coef, texts, preferred_element_type=jnp.float32)

    def over_images(coef, pictures):
        return lax.dot_general(coef, pictures, (((0,), (0,)), ((), ())), preferred_element_type=jnp.float32)

    pictures = jnp.concatenate(images)
    texts = jnp.concatenate([text0, text1, text2])
    logits = scores(pictures, texts)
    place = lax.broadcasted_iota(jnp.int32, logits.shape, 0)
    column = lax.broadcasted_iota(jnp.int32, logits.shape, 1)
    turn, which = place // ROWS, column // ROWS
    i = (k - turn + LINE) % LINE
    used = jnp.where(which == 0, i >= k, jnp.where(which == 1, True, i <= k + 1))
    wanted = jnp.concatenate([positive_caption_indices - here * ROWS, jnp.full((2 * ROWS,), -1, jnp.int32)])
    positive = wanted[:, None] == column
    tempered = scale * logits + shift
    sign = jnp.where(positive, -1.0, 1.0).astype(jnp.float32)
    coef = jnp.where(used, scale * sign * jax.nn.sigmoid(sign * tempered), 0.0).astype(LOW)
    coef3 = jnp.where(k == 2, negatives(scores(images[2], text3)), 0.0).astype(LOW)

    grad_texts = over_images(coef, pictures)
    grad_far = over_images(coef3, images[2])
    grad_images = over_texts(coef, texts)
    back = [
        line_turned(grad_images[ROWS : 2 * ROWS].astype(LOW), -1),
        line_turned((grad_images[2 * ROWS :] + over_texts(coef3, text3)).astype(LOW), -2),
    ]
    pair = jnp.stack([grad_texts[ROWS : 2 * ROWS].astype(LOW), grad_far.astype(LOW)])
    pair = sent(pair, lambda b: b + LINE if b // LINE % 2 == 0 else b - LINE).astype(jnp.float32)
    own = jnp.where(core == 0, pair[0], 0.0)
    earlier = grad_texts[2 * ROWS :] + jnp.where(core == 0, jnp.where(k == 2, pair[1], 0.0), pair[0])
    earlier = group_back(earlier.astype(LOW), y).astype(jnp.float32)
    far_back = sent(grad_far.astype(LOW), lambda b: b - 3 * LINE if b % GROUP == 2 else None).astype(jnp.float32)
    far_back = jnp.where(here % GROUP == 5, far_back, 0.0)
    grad_image = grad_images[:ROWS] + (back[0].astype(jnp.float32) + back[1].astype(jnp.float32))
    grad_text = grad_texts[:ROWS] + own + earlier + far_back
    return grad_image, grad_text


def solution(mesh):
    in_specs = (P(AXES, None), P(AXES, None), P(AXES), P(), P())
    out_specs = (P(AXES, None), P(AXES, None))
    return jax.shard_map(
        on_device, mesh=mesh, in_specs=in_specs, out_specs=out_specs, check_vma=False
    )
```

```python
import jax
import jax.numpy as jnp
from jax import lax
from jax.experimental import pallas as pl
from jax.experimental.pallas import tpu as pltpu
from jax.sharding import PartitionSpec as P

AXES = ("dp", "mp")
ROWS = 192
D = 1152
LINE = 3
GROUP = 6
LAP = 8
NB = 768
LOW = jnp.bfloat16
F32 = jnp.float32


def lap_of(b):
    return (b // GROUP) % LAP


def core_of(b):
    return b // LINE % 2


def sent(value, target):
    pairs = [(b, target(b) % NB) for b in range(NB) if target(b) is not None]
    return lax.ppermute(value, AXES, pairs)


def line_turned(value, by):
    return sent(value, lambda b: b // LINE * LINE + (b + by) % LINE)


def cores_swapped(value):
    return sent(value, lambda b: b + LINE if core_of(b) == 0 else b - LINE)


def plane(b, by):
    step = b % LINE if core_of(b) == 0 else GROUP - 1 - b % LINE
    return step if by > 0 else LAP - 1 - step


def detour(value, by):
    start = LAP - 1 if by > 0 else 0
    return sent(value, lambda b: b + GROUP * (plane(b, by) - start) if lap_of(b) == start else None)


def after_detour(value, by):
    end = 0 if by > 0 else LAP - 1
    return sent(value, lambda b: b + GROUP * (by * LAP + end - lap_of(b)) if lap_of(b) == plane(b, by) else None)


def straight(value, by):
    start = LAP - 1 if by > 0 else 0
    return sent(value, lambda b: None if lap_of(b) == start else b + by * GROUP)


def scores(texts, pictures):
    return lax.dot_general(texts, pictures, (((1,), (1,)), ((), ())), preferred_element_type=F32)


def matmul(a, b):
    return jnp.dot(a, b, preferred_element_type=F32)


def own_texts(k_ref, scale_ref, shift_ref, wanted, i0, i1, i2, t0, pictures, coef, gt0):
    scale, shift, k = scale_ref[0], shift_ref[0], k_ref[0]
    pictures[0:ROWS] = i0[...]
    pictures[ROWS : 2 * ROWS] = i1[...]
    pictures[2 * ROWS :] = i2[...]
    logits = scores(t0[...], pictures[...])
    row = lax.broadcasted_iota(jnp.int32, logits.shape, 0)
    column = lax.broadcasted_iota(jnp.int32, logits.shape, 1)
    sign = jnp.where(wanted[...] == row, -1.0, 1.0).astype(F32)
    value = scale * sign * jax.nn.sigmoid(sign * (scale * logits + shift))
    one = (column >= ROWS) & (column < 2 * ROWS)
    unused = (one & (k != 0)) | ((column >= 2 * ROWS) & (k == 2))
    coef[...] = jnp.where(unused, 0.0, value).astype(LOW)
    gt0[...] = matmul(coef[...], pictures[...])


def over_texts(coef, texts):
    return lax.dot_general(coef, texts, (((0,), (0,)), ((), ())), preferred_element_type=F32)


def other_texts(
    k_ref, core_ref, scale_ref, shift_ref, near, crossed, t2, t0, i2, pictures, coef0,
    pair, gt2, gi0, gi1, gi2, texts, coef,
):
    scale, shift, k, core = scale_ref[0], shift_ref[0], k_ref[0], core_ref[0]
    texts[ROWS : 2 * ROWS] = t2[...]
    texts[2 * ROWS :] = t0[...]
    coef[2 * ROWS :] = coef0[...]

    @pl.when(core == 0)
    def _():
        texts[0:ROWS] = crossed[...]

    @pl.when(core != 0)
    def _():
        texts[0:ROWS] = near[...]

    two = slice(0, 2 * ROWS)
    logits = scores(texts[two], pictures[...])
    row = lax.broadcasted_iota(jnp.int32, logits.shape, 0)
    column = lax.broadcasted_iota(jnp.int32, logits.shape, 1)
    value = scale * jax.nn.sigmoid(scale * logits + shift)
    unused = (row >= ROWS) & (column >= ROWS) & (column < 2 * ROWS) & (k == 0)
    coef[two] = jnp.where(unused, 0.0, value).astype(LOW)
    by_text = matmul(coef[two], pictures[...])
    pair[0] = by_text[0:ROWS].astype(LOW)
    gt2[...] = by_text[ROWS:]
    by_image = over_texts(coef[...], texts[...])
    gi0[...] = by_image[0:ROWS]
    gi1[...] = by_image[ROWS : 2 * ROWS].astype(LOW)

    @pl.when(k != 2)
    def _():
        gi2[...] = by_image[2 * ROWS :].astype(LOW)
        pair[1] = jnp.zeros((ROWS, D), LOW)

    def with_far(t3):
        far = (scale * jax.nn.sigmoid(scale * scores(t3[...], i2[...]) + shift)).astype(LOW)
        pair[1] = matmul(far, i2[...]).astype(LOW)
        gi2[...] = (by_image[2 * ROWS :] + over_texts(far, t3[...])).astype(LOW)

    @pl.when((k == 2) & (core == 0))
    def _():
        with_far(near)

    @pl.when((k == 2) & (core != 0))
    def _():
        with_far(crossed)


def kernel_call(body, n_small, args, outs, scratch=()):
    return pl.pallas_call(
        body,
        out_shape=[jax.ShapeDtypeStruct(shape, kind) for shape, kind in outs],
        in_specs=[pl.BlockSpec(memory_space=pltpu.SMEM)] * n_small
        + [pl.BlockSpec(memory_space=pltpu.VMEM)] * (len(args) - n_small),
        out_specs=[pl.BlockSpec(memory_space=pltpu.VMEM)] * len(outs),
        scratch_shapes=[pltpu.VMEM(shape, LOW) for shape in scratch],
        compiler_params=pltpu.CompilerParams(vmem_limit_bytes=12 * 1024 * 1024),
    )(*args)


def on_device(
    picture_embedding_matrix,
    caption_embedding_matrix,
    positive_caption_indices,
    sharpness_multiplier,
    additive_shift_term,
):
    here = lax.axis_index(AXES)
    k = here % LINE
    core = core_of(here)
    y = lap_of(here)
    image0, text0 = picture_embedding_matrix, caption_embedding_matrix
    small = [k.astype(jnp.int32).reshape(1), sharpness_multiplier, additive_shift_term]
    wanted = jnp.concatenate([positive_caption_indices - here * ROWS, jnp.full((2 * ROWS,), -1, jnp.int32)])[None]
    block, three = (ROWS, D), LINE * ROWS

    corner = detour(text0, 1)
    main = straight(text0, 1)
    image1 = line_turned(image0, 1)
    image2 = line_turned(image0, 2)
    near = sent(text0, lambda b: b + LINE if core_of(b) == 0 else (b + 3 * LINE if b % GROUP == 5 else None))
    relayed = after_detour(corner, 1)
    image1, image2, near, main, relayed = lax.optimization_barrier((image1, image2, near, main, relayed))
    pictures, coef0, gt0 = kernel_call(
        own_texts,
        3,
        small + [wanted, image0, image1, image2, text0],
        [((three, D), LOW), ((ROWS, three), LOW), (block, F32)],
    )
    text2 = jnp.where(y == 0, relayed, main)
    crossed = cores_swapped(text2)
    pair, gt2, gi0, gi1, gi2 = kernel_call(
        other_texts,
        4,
        [small[0], core.astype(jnp.int32).reshape(1), *small[1:], near, crossed, text2, text0, image2, pictures, coef0],
        [((2, ROWS, D), LOW), (block, F32), (block, F32), (block, LOW), (block, LOW)],
        [(three, D), (three, three)],
    )
    other = cores_swapped(pair)
    earlier = (gt2 + jnp.where(core == 0, other[1], other[0]).astype(F32)).astype(LOW)
    back_corner = detour(earlier, -1)
    back_main = straight(earlier, -1)
    far = sent(pair[1], lambda b: b - 3 * LINE if b % GROUP == 2 else None)
    back1 = line_turned(gi1, -1)
    back2 = line_turned(gi2, -2)
    back_relayed = after_detour(back_corner, -1)
    back_text = jnp.where(y == LAP - 1, back_relayed, back_main)
    rest = jnp.where(core == 0, other[0].astype(F32), jnp.where(k == 2, far.astype(F32), 0.0))
    grad_text = gt0 + rest + back_text.astype(F32)
    grad_image = gi0 + (back1.astype(F32) + back2.astype(F32))
    return grad_image, grad_text


def solution(mesh):
    in_specs = (P(AXES, None), P(AXES, None), P(AXES), P(), P())
    out_specs = (P(AXES, None), P(AXES, None))
    return jax.shard_map(
        on_device, mesh=mesh, in_specs=in_specs, out_specs=out_specs, check_vma=False
    )
```

```python
import jax
import jax.numpy as jnp
from jax import lax
from jax.experimental import pallas as pl
from jax.experimental.pallas import tpu as pltpu
from jax.sharding import PartitionSpec as P

AXES = ("dp", "mp")
ROWS = 192
D = 1152
LINE = 3
GROUP = 6
LAP = 8
LAPS = 4
NB = 768
LOW = jnp.bfloat16
F32 = jnp.float32


def lap_of(b):
    return (b // GROUP) % LAP


def core_of(b):
    return b // LINE % 2


def sent(value, target):
    pairs = [(b, target(b) % NB) for b in range(NB) if target(b) is not None]
    return lax.ppermute(value, AXES, pairs)


def line_turned(value, by):
    return sent(value, lambda b: b // LINE * LINE + (b + by) % LINE)


def cores_swapped(value):
    return sent(value, lambda b: b + LINE if core_of(b) == 0 else b - LINE)


def plane(b, by):
    step = b % LINE if core_of(b) == 0 else GROUP - 1 - b % LINE
    return step if by > 0 else LAP - 1 - step


def at(x, lap, y, place):
    return ((x % LAPS * LAPS + lap % LAPS) * LAP + y) * GROUP + place


def detour(value, by):
    start, last = (LAP - 1, LAPS - 1) if by > 0 else (0, 0)

    def target(b):
        x, lap = b // (GROUP * LAP * LAPS), b // (GROUP * LAP) % LAPS
        return at(x + (by if lap == last else 0), lap, plane(b, by), b % GROUP) if lap_of(b) == start else None

    return sent(value, target)


def after_detour(value, by):
    end = 0 if by > 0 else LAP - 1

    def target(b):
        x, lap = b // (GROUP * LAP * LAPS), b // (GROUP * LAP) % LAPS
        return at(x, lap + by, end, b % GROUP) if lap_of(b) == plane(b, by) else None

    return sent(value, target)


def straight(value, by):
    start = LAP - 1 if by > 0 else 0
    return sent(value, lambda b: None if lap_of(b) == start else b + by * GROUP)


def scores(texts, pictures):
    return lax.dot_general(texts, pictures, (((1,), (1,)), ((), ())), preferred_element_type=F32)


def matmul(a, b):
    return jnp.dot(a, b, preferred_element_type=F32)


def own_texts(k_ref, scale_ref, shift_ref, wanted, i0, i1, i2, t0, coef, gt0, pictures):
    scale, shift, k = scale_ref[0], shift_ref[0], k_ref[0]
    pictures[0:ROWS] = i0[...]
    pictures[ROWS : 2 * ROWS] = i1[...]
    pictures[2 * ROWS :] = i2[...]
    logits = scores(t0[...], pictures[...])
    row = lax.broadcasted_iota(jnp.int32, logits.shape, 0)
    column = lax.broadcasted_iota(jnp.int32, logits.shape, 1)
    sign = jnp.where(wanted[...] == row, -1.0, 1.0).astype(F32)
    value = scale * sign * jax.nn.sigmoid(sign * (scale * logits + shift))
    one = (column >= ROWS) & (column < 2 * ROWS)
    unused = (one & (k != 0)) | ((column >= 2 * ROWS) & (k == 2))
    coef[...] = jnp.where(unused, 0.0, value).astype(LOW)
    gt0[...] = matmul(coef[...], pictures[...])


def over_texts(coef, texts):
    return lax.dot_general(coef, texts, (((0,), (0,)), ((), ())), preferred_element_type=F32)


def over_texts(coef, texts):
    return lax.dot_general(coef, texts, (((0,), (0,)), ((), ())), preferred_element_type=F32)


def other_texts(
    k_ref, core_ref, scale_ref, shift_ref, t0, t2, far, i0, i1, i2, o1, o02, coef0, gt0p,
    ours, theirs, share, gt0, far_share, texts, coef, spare, others, pictures,
):
    scale, shift, k, core = scale_ref[0], shift_ref[0], k_ref[0], core_ref[0]

    def negatives(some_texts, some_pictures):
        return scale * jax.nn.sigmoid(scale * scores(some_texts, some_pictures) + shift)

    texts[0:ROWS] = t2[...]
    texts[ROWS:] = t0[...]
    coef[ROWS:] = coef0[...]
    pictures[0:ROWS] = i0[...]
    pictures[ROWS : 2 * ROWS] = i1[...]
    pictures[2 * ROWS :] = i2[...]
    others[0:ROWS] = o02[0]
    others[ROWS : 2 * ROWS] = o1[...]
    others[2 * ROWS :] = o02[1]

    @pl.when(core == 0)
    def _():
        spare[...] = t0[...]

    @pl.when(core != 0)
    def _():
        spare[...] = t2[...]

    value = negatives(t2[...], pictures[...])
    column = lax.broadcasted_iota(jnp.int32, value.shape, 1)
    unused = (column >= ROWS) & (column < 2 * ROWS) & (k == 0)
    coef[0:ROWS] = jnp.where(unused, 0.0, value).astype(LOW)
    full = negatives(spare[...], others[...]).astype(LOW)
    by_far_text = matmul(coef[0:ROWS], pictures[...])
    by_text = matmul(full, others[...])
    ours[...] = over_texts(coef[...], texts[...])
    by_image = over_texts(full, spare[...])
    theirs[0 : 2 * ROWS] = by_image[0 : 2 * ROWS].astype(LOW)

    @pl.when(k != 2)
    def _():
        theirs[2 * ROWS :] = by_image[2 * ROWS :].astype(LOW)

    def with_seventh(text):
        single = negatives(text[...], others[2 * ROWS :]).astype(LOW)
        theirs[2 * ROWS :] = (by_image[2 * ROWS :] + over_texts(single, text[...])).astype(LOW)
        return matmul(single, others[2 * ROWS :])

    @pl.when((core == 0) & (k != 2))
    def _():
        gt0[...] = gt0p[...] + by_text
        share[...] = by_far_text.astype(LOW)

    @pl.when((core == 0) & (k == 2))
    def _():
        gt0[...] = gt0p[...] + by_text
        share[...] = (by_far_text + with_seventh(t2)).astype(LOW)

    @pl.when(core != 0)
    def _():
        gt0[...] = gt0p[...]
        share[...] = (by_far_text + by_text).astype(LOW)

    @pl.when((core != 0) & (k == 2))
    def _():
        far_share[...] = with_seventh(far).astype(LOW)

    @pl.when((core == 0) | (k != 2))
    def _():
        far_share[...] = jnp.zeros((ROWS, D), LOW)


def both_cores(ours, received, gi0, gi1, gi2):
    gi0[...] = ours[0:ROWS] + received[0:ROWS].astype(F32)
    gi1[...] = (ours[ROWS : 2 * ROWS] + received[ROWS : 2 * ROWS].astype(F32)).astype(LOW)
    gi2[...] = (ours[2 * ROWS :] + received[2 * ROWS :].astype(F32)).astype(LOW)


def line_total(gu0, back1, back2, grad_text):
    grad_text[...] = gu0[...] + (back1[...].astype(F32) + back2[...].astype(F32))


def shift_total(late_ref, far_ref, gv0, main, relayed, far, grad_picture):
    returned = jnp.where(late_ref[0] != 0, relayed[...], main[...]).astype(F32)
    grad_picture[...] = gv0[...] + (returned + jnp.where(far_ref[0] != 0, far[...].astype(F32), 0.0))


def kernel_call(body, n_small, args, outs, scratch=(), flops=0):
    return pl.pallas_call(
        body,
        out_shape=[jax.ShapeDtypeStruct(shape, kind) for shape, kind in outs],
        in_specs=[pl.BlockSpec(memory_space=pltpu.SMEM)] * n_small
        + [pl.BlockSpec(memory_space=pltpu.VMEM)] * (len(args) - n_small),
        out_specs=[pl.BlockSpec(memory_space=pltpu.VMEM)] * len(outs),
        cost_estimate=pl.CostEstimate(flops=flops, bytes_accessed=0, transcendentals=0) if flops else None,
        scratch_shapes=[pltpu.VMEM(shape, LOW) for shape in scratch],
        compiler_params=pltpu.CompilerParams(vmem_limit_bytes=12 * 1024 * 1024),
    )(*args)


def on_device(
    picture_embedding_matrix,
    caption_embedding_matrix,
    positive_caption_indices,
    sharpness_multiplier,
    additive_shift_term,
):
    here = lax.axis_index(AXES)
    k = here % LINE
    core = core_of(here)
    y = lap_of(here)
    image0, text0 = picture_embedding_matrix, caption_embedding_matrix
    small = [k.astype(jnp.int32).reshape(1), sharpness_multiplier, additive_shift_term]
    wanted = jnp.concatenate([positive_caption_indices - here * ROWS, jnp.full((2 * ROWS,), -1, jnp.int32)])[None]
    block, three = (ROWS, D), LINE * ROWS

    corner = detour(text0, 1)
    main = straight(text0, 1)
    image1 = line_turned(image0, 1)
    image2 = line_turned(image0, 2)
    far = sent(text0, lambda b: b + 2 * GROUP if b % GROUP == 5 else None)
    relayed = after_detour(corner, 1)
    others = [cores_swapped(image1), cores_swapped(jnp.stack([image0, image2]))]
    raw = image1, image2
    image1, image2, main, far, relayed = lax.optimization_barrier((image1, image2, main, far, relayed))
    coef0, gt0 = kernel_call(
        own_texts,
        3,
        small + [wanted, image0, *raw, text0],
        [((ROWS, three), LOW), (block, F32)],
        [(three, D)],
    )
    text2 = jnp.where(y == 0, relayed, main)
    ours, theirs, share, gt0, far = kernel_call(
        other_texts,
        4,
        [small[0], core.astype(jnp.int32).reshape(1), *small[1:], text0, text2, far, image0, image1, image2, *others, coef0, gt0],
        [((three, D), F32), ((three, D), LOW), (block, LOW), (block, F32), (block, LOW)],
        [(2 * ROWS, D), (2 * ROWS, three), (ROWS, D), (three, D), (three, D)],
    )
    received = cores_swapped(theirs)
    back_corner = detour(share, -1)
    back_main = straight(share, -1)
    gi0, gi1, gi2 = kernel_call(
        both_cores, 0, [ours, received], [(block, F32), (block, LOW), (block, LOW)]
    )
    far_back = sent(far, lambda b: b - 2 * GROUP if b % GROUP == 5 else None)
    back1 = line_turned(gi1, -1)
    back2 = line_turned(gi2, -2)
    back_relayed = after_detour(back_corner, -1)
    [grad_image] = kernel_call(line_total, 0, [gi0, back1, back2], [(block, F32)], flops=20_000_000_000)
    grad_image, gt0 = lax.optimization_barrier((grad_image, gt0))
    flag = lambda value: value.astype(jnp.int32).reshape(1)
    [grad_text] = kernel_call(
        shift_total,
        2,
        [flag(y == LAP - 1), flag(here % GROUP == 5), gt0, back_main, back_relayed, far_back],
        [(block, F32)],
    )
    return grad_image, grad_text


def solution(mesh):
    in_specs = (P(AXES, None), P(AXES, None), P(AXES), P(), P())
    out_specs = (P(AXES, None), P(AXES, None))
    return jax.shard_map(
        on_device, mesh=mesh, in_specs=in_specs, out_specs=out_specs, check_vma=False
    )
```

```python
import jax
import jax.numpy as jnp
from jax import lax
from jax.experimental import pallas as pl
from jax.experimental.pallas import tpu as pltpu
from jax.sharding import PartitionSpec as P

AXES = ("dp", "mp")
ROWS = 192
D = 1152
LINE = 3
GROUP = 6
LAP = 8
LAPS = 4
NB = 768
LOW = jnp.bfloat16
F32 = jnp.float32


def lap_of(b):
    return (b // GROUP) % LAP


def core_of(b):
    return b // LINE % 2


def sent(value, target):
    pairs = [(b, target(b) % NB) for b in range(NB) if target(b) is not None]
    return lax.ppermute(value, AXES, pairs)


def line_turned(value, by):
    return sent(value, lambda b: b // LINE * LINE + (b + by) % LINE)


def cores_swapped(value):
    return sent(value, lambda b: b + LINE if core_of(b) == 0 else b - LINE)


def plane(b, by):
    step = b % LINE if core_of(b) == 0 else GROUP - 1 - b % LINE
    return step if by > 0 else LAP - 1 - step


def at(x, lap, y, place):
    return ((x % LAPS * LAPS + lap % LAPS) * LAP + y) * GROUP + place


def detour(value, by):
    start, last = (LAP - 1, LAPS - 1) if by > 0 else (0, 0)

    def target(b):
        x, lap = b // (GROUP * LAP * LAPS), b // (GROUP * LAP) % LAPS
        return at(x + (by if lap == last else 0), lap, plane(b, by), b % GROUP) if lap_of(b) == start else None

    return sent(value, target)


def after_detour(value, by):
    end = 0 if by > 0 else LAP - 1

    def target(b):
        x, lap = b // (GROUP * LAP * LAPS), b // (GROUP * LAP) % LAPS
        return at(x, lap + by, end, b % GROUP) if lap_of(b) == plane(b, by) else None

    return sent(value, target)


def straight(value, by):
    start = LAP - 1 if by > 0 else 0
    return sent(value, lambda b: None if lap_of(b) == start else b + by * GROUP)


def scores(texts, pictures):
    return lax.dot_general(texts, pictures, (((1,), (1,)), ((), ())), preferred_element_type=F32)


def matmul(a, b):
    return jnp.dot(a, b, preferred_element_type=F32)


def own_texts(k_ref, scale_ref, shift_ref, wanted, i0, i1, i2, t0, coef, gt0, pictures):
    scale, shift, k = scale_ref[0], shift_ref[0], k_ref[0]
    pictures[0:ROWS] = i0[...]
    pictures[ROWS : 2 * ROWS] = i1[...]
    pictures[2 * ROWS :] = i2[...]
    logits = scores(t0[...], pictures[...])
    row = lax.broadcasted_iota(jnp.int32, logits.shape, 0)
    column = lax.broadcasted_iota(jnp.int32, logits.shape, 1)
    sign = jnp.where(wanted[...] == row, -1.0, 1.0).astype(F32)
    value = scale * sign * jax.nn.sigmoid(sign * (scale * logits + shift))
    one = (column >= ROWS) & (column < 2 * ROWS)
    unused = (one & (k != 0)) | ((column >= 2 * ROWS) & (k == 2))
    coef[...] = jnp.where(unused, 0.0, value).astype(LOW)
    gt0[...] = matmul(coef[...], pictures[...])


def over_texts(coef, texts):
    return lax.dot_general(coef, texts, (((0,), (0,)), ((), ())), preferred_element_type=F32)


def over_texts(coef, texts):
    return lax.dot_general(coef, texts, (((0,), (0,)), ((), ())), preferred_element_type=F32)


def negatives(texts, pictures, scale_ref, shift_ref):
    scale, shift = scale_ref[0], shift_ref[0]
    return scale * jax.nn.sigmoid(scale * scores(texts, pictures) + shift)


def other_line(
    k_ref, core_ref, scale_ref, shift_ref, t0, t2, far, o1, o02,
    theirs, own_part, share_part, far_share, spare, others,
):
    k, core = k_ref[0], core_ref[0]
    others[0:ROWS] = o02[0]
    others[ROWS : 2 * ROWS] = o1[...]
    others[2 * ROWS :] = o02[1]

    @pl.when(core == 0)
    def _():
        spare[...] = t0[...]

    @pl.when(core != 0)
    def _():
        spare[...] = t2[...]

    full = negatives(spare[...], others[...], scale_ref, shift_ref).astype(LOW)
    by_image = over_texts(full, spare[...])
    theirs[0 : 2 * ROWS] = by_image[0 : 2 * ROWS].astype(LOW)
    by_text = matmul(full, others[...])

    @pl.when(k != 2)
    def _():
        theirs[2 * ROWS :] = by_image[2 * ROWS :].astype(LOW)

    def with_seventh(text):
        single = negatives(text[...], others[2 * ROWS :], scale_ref, shift_ref).astype(LOW)
        theirs[2 * ROWS :] = (by_image[2 * ROWS :] + over_texts(single, text[...])).astype(LOW)
        return matmul(single, others[2 * ROWS :])

    @pl.when(core == 0)
    def _():
        own_part[...] = by_text

    @pl.when(core != 0)
    def _():
        own_part[...] = jnp.zeros((ROWS, D), F32)
        share_part[...] = by_text

    @pl.when((core == 0) & (k != 2))
    def _():
        share_part[...] = jnp.zeros((ROWS, D), F32)

    @pl.when((core == 0) & (k == 2))
    def _():
        share_part[...] = with_seventh(t2)

    @pl.when((core != 0) & (k == 2))
    def _():
        far_share[...] = with_seventh(far).astype(LOW)

    @pl.when((core == 0) | (k != 2))
    def _():
        far_share[...] = jnp.zeros((ROWS, D), LOW)


def own_line(
    k_ref, scale_ref, shift_ref, t0, t2, i0, i1, i2, coef0, gt0p, own_part, share_part,
    ours, share, gt0, texts, coef, pictures,
):
    k = k_ref[0]
    texts[0:ROWS] = t2[...]
    texts[ROWS:] = t0[...]
    coef[ROWS:] = coef0[...]
    pictures[0:ROWS] = i0[...]
    pictures[ROWS : 2 * ROWS] = i1[...]
    pictures[2 * ROWS :] = i2[...]
    value = negatives(t2[...], pictures[...], scale_ref, shift_ref)
    column = lax.broadcasted_iota(jnp.int32, value.shape, 1)
    unused = (column >= ROWS) & (column < 2 * ROWS) & (k == 0)
    coef[0:ROWS] = jnp.where(unused, 0.0, value).astype(LOW)
    share[...] = (share_part[...] + matmul(coef[0:ROWS], pictures[...])).astype(LOW)
    ours[...] = over_texts(coef[...], texts[...])
    gt0[...] = gt0p[...] + own_part[...]


def both_cores(ours, received, gi0, gi1, gi2):
    gi0[...] = ours[0:ROWS] + received[0:ROWS].astype(F32)
    gi1[...] = (ours[ROWS : 2 * ROWS] + received[ROWS : 2 * ROWS].astype(F32)).astype(LOW)
    gi2[...] = (ours[2 * ROWS :] + received[2 * ROWS :].astype(F32)).astype(LOW)


def line_total(gu0, back1, back2, grad_text):
    grad_text[...] = gu0[...] + (back1[...].astype(F32) + back2[...].astype(F32))


def shift_total(late_ref, far_ref, gv0, main, relayed, far, grad_picture):
    returned = jnp.where(late_ref[0] != 0, relayed[...], main[...]).astype(F32)
    grad_picture[...] = gv0[...] + (returned + jnp.where(far_ref[0] != 0, far[...].astype(F32), 0.0))


def kernel_call(body, n_small, args, outs, scratch=(), flops=0):
    return pl.pallas_call(
        body,
        out_shape=[jax.ShapeDtypeStruct(shape, kind) for shape, kind in outs],
        in_specs=[pl.BlockSpec(memory_space=pltpu.SMEM)] * n_small
        + [pl.BlockSpec(memory_space=pltpu.VMEM)] * (len(args) - n_small),
        out_specs=[pl.BlockSpec(memory_space=pltpu.VMEM)] * len(outs),
        cost_estimate=pl.CostEstimate(flops=flops, bytes_accessed=0, transcendentals=0) if flops else None,
        scratch_shapes=[pltpu.VMEM(shape, LOW) for shape in scratch],
        compiler_params=pltpu.CompilerParams(vmem_limit_bytes=12 * 1024 * 1024),
    )(*args)


def on_device(
    picture_embedding_matrix,
    caption_embedding_matrix,
    positive_caption_indices,
    sharpness_multiplier,
    additive_shift_term,
):
    here = lax.axis_index(AXES)
    k = here % LINE
    core = core_of(here)
    y = lap_of(here)
    image0, text0 = picture_embedding_matrix, caption_embedding_matrix
    small = [k.astype(jnp.int32).reshape(1), sharpness_multiplier, additive_shift_term]
    wanted = jnp.concatenate([positive_caption_indices - here * ROWS, jnp.full((2 * ROWS,), -1, jnp.int32)])[None]
    block, three = (ROWS, D), LINE * ROWS

    corner = detour(text0, 1)
    main = straight(text0, 1)
    image1 = line_turned(image0, 1)
    image2 = line_turned(image0, 2)
    far = sent(text0, lambda b: b + 2 * GROUP if b % GROUP == 5 else None)
    relayed = after_detour(corner, 1)
    others = [cores_swapped(image1), cores_swapped(jnp.stack([image0, image2]))]
    raw = image1, image2
    image1, image2, main, far, relayed = lax.optimization_barrier((image1, image2, main, far, relayed))
    coef0, gt0 = kernel_call(
        own_texts,
        3,
        small + [wanted, image0, *raw, text0],
        [((ROWS, three), LOW), (block, F32)],
        [(three, D)],
    )
    text2 = jnp.where(y == 0, relayed, main)
    coef0, far = lax.optimization_barrier((coef0, far))
    theirs, own_part, share_part, far = kernel_call(
        other_line,
        4,
        [small[0], core.astype(jnp.int32).reshape(1), *small[1:], text0, text2, far, *others],
        [((three, D), LOW), (block, F32), (block, F32), (block, LOW)],
        [(ROWS, D), (three, D)],
    )
    ours, share, gt0 = kernel_call(
        own_line,
        3,
        [*small, text0, text2, image0, image1, image2, coef0, gt0, own_part, share_part],
        [((three, D), F32), (block, LOW), (block, F32)],
        [(2 * ROWS, D), (2 * ROWS, three), (three, D)],
    )
    received = cores_swapped(theirs)
    back_corner = detour(share, -1)
    back_main = straight(share, -1)
    gi0, gi1, gi2 = kernel_call(
        both_cores, 0, [ours, received], [(block, F32), (block, LOW), (block, LOW)]
    )
    far_back = sent(far, lambda b: b - 2 * GROUP if b % GROUP == 5 else None)
    back1 = line_turned(gi1, -1)
    back2 = line_turned(gi2, -2)
    back_relayed = after_detour(back_corner, -1)
    [grad_image] = kernel_call(line_total, 0, [gi0, back1, back2], [(block, F32)], flops=20_000_000_000)
    grad_image, gt0 = lax.optimization_barrier((grad_image, gt0))
    flag = lambda value: value.astype(jnp.int32).reshape(1)
    [grad_text] = kernel_call(
        shift_total,
        2,
        [flag(y == LAP - 1), flag(here % GROUP == 5), gt0, back_main, back_relayed, far_back],
        [(block, F32)],
    )
    return grad_image, grad_text


def solution(mesh):
    in_specs = (P(AXES, None), P(AXES, None), P(AXES), P(), P())
    out_specs = (P(AXES, None), P(AXES, None))
    return jax.shard_map(
        on_device, mesh=mesh, in_specs=in_specs, out_specs=out_specs, check_vma=False
    )
```

```python
import jax
import jax.numpy as jnp
from jax import lax
from jax.experimental import pallas as pl
from jax.experimental.pallas import tpu as pltpu
from jax.sharding import PartitionSpec as P

AXES = ("dp", "mp")
ROWS = 192
D = 1152
LINE = 3
GROUP = 6
LAP = 8
LAPS = 4
NB = 768
LOW = jnp.bfloat16
F32 = jnp.float32


def lap_of(b):
    return (b // GROUP) % LAP


def core_of(b):
    return b // LINE % 2


def sent(value, target):
    pairs = [(b, target(b) % NB) for b in range(NB) if target(b) is not None]
    return lax.ppermute(value, AXES, pairs)


def line_turned(value, by):
    return sent(value, lambda b: b // LINE * LINE + (b + by) % LINE)


def cores_swapped(value):
    return sent(value, lambda b: b + LINE if core_of(b) == 0 else b - LINE)


def plane(b, by):
    step = b % LINE if core_of(b) == 0 else GROUP - 1 - b % LINE
    return step if by > 0 else LAP - 1 - step


def at(x, lap, y, place):
    return ((x % LAPS * LAPS + lap % LAPS) * LAP + y) * GROUP + place


def detour(value, by):
    start, last = (LAP - 1, LAPS - 1) if by > 0 else (0, 0)

    def target(b):
        x, lap = b // (GROUP * LAP * LAPS), b // (GROUP * LAP) % LAPS
        return at(x + (by if lap == last else 0), lap, plane(b, by), b % GROUP) if lap_of(b) == start else None

    return sent(value, target)


def after_detour(value, by):
    end = 0 if by > 0 else LAP - 1

    def target(b):
        x, lap = b // (GROUP * LAP * LAPS), b // (GROUP * LAP) % LAPS
        return at(x, lap + by, end, b % GROUP) if lap_of(b) == plane(b, by) else None

    return sent(value, target)


def straight(value, by):
    start = LAP - 1 if by > 0 else 0
    return sent(value, lambda b: None if lap_of(b) == start else b + by * GROUP)


def scores(texts, pictures):
    return lax.dot_general(texts, pictures, (((1,), (1,)), ((), ())), preferred_element_type=F32)


def matmul(a, b):
    return jnp.dot(a, b, preferred_element_type=F32)


def own_texts(k_ref, scale_ref, shift_ref, wanted, i0, i1, i2, t0, coef, gt0, pictures):
    scale, shift, k = scale_ref[0], shift_ref[0], k_ref[0]
    pictures[0:ROWS] = i0[...]
    pictures[ROWS : 2 * ROWS] = i1[...]
    pictures[2 * ROWS :] = i2[...]
    logits = scores(t0[...], pictures[...])
    row = lax.broadcasted_iota(jnp.int32, logits.shape, 0)
    column = lax.broadcasted_iota(jnp.int32, logits.shape, 1)
    sign = jnp.where(wanted[...] == row, -1.0, 1.0).astype(F32)
    value = scale * sign * jax.nn.sigmoid(sign * (scale * logits + shift))
    one = (column >= ROWS) & (column < 2 * ROWS)
    unused = (one & (k != 0)) | ((column >= 2 * ROWS) & (k == 2))
    coef[...] = jnp.where(unused, 0.0, value).astype(LOW)
    gt0[...] = matmul(coef[...], pictures[...])


def over_texts(coef, texts):
    return lax.dot_general(coef, texts, (((0,), (0,)), ((), ())), preferred_element_type=F32)


def over_texts(coef, texts):
    return lax.dot_general(coef, texts, (((0,), (0,)), ((), ())), preferred_element_type=F32)


def negatives(texts, pictures, scale_ref, shift_ref):
    scale, shift = scale_ref[0], shift_ref[0]
    return scale * jax.nn.sigmoid(scale * scores(texts, pictures) + shift)


def other_line(
    k_ref, core_ref, scale_ref, shift_ref, t0, t2, far, o1, o02,
    theirs, own_part, share_part, far_share, spare, others,
):
    k, core = k_ref[0], core_ref[0]
    others[0:ROWS] = o02[0]
    others[ROWS : 2 * ROWS] = o1[...]
    others[2 * ROWS :] = o02[1]

    @pl.when(core == 0)
    def _():
        spare[...] = t0[...]

    @pl.when(core != 0)
    def _():
        spare[...] = t2[...]

    full = negatives(spare[...], others[...], scale_ref, shift_ref).astype(LOW)
    by_image = over_texts(full, spare[...])
    theirs[0 : 2 * ROWS] = by_image[0 : 2 * ROWS].astype(LOW)
    by_text = matmul(full, others[...])

    @pl.when(k != 2)
    def _():
        theirs[2 * ROWS :] = by_image[2 * ROWS :].astype(LOW)

    def with_seventh(text):
        single = negatives(text[...], others[2 * ROWS :], scale_ref, shift_ref).astype(LOW)
        theirs[2 * ROWS :] = (by_image[2 * ROWS :] + over_texts(single, text[...])).astype(LOW)
        return matmul(single, others[2 * ROWS :])

    @pl.when(core == 0)
    def _():
        own_part[...] = by_text

    @pl.when(core != 0)
    def _():
        own_part[...] = jnp.zeros((ROWS, D), F32)
        share_part[...] = by_text

    @pl.when((core == 0) & (k != 2))
    def _():
        share_part[...] = jnp.zeros((ROWS, D), F32)

    @pl.when((core == 0) & (k == 2))
    def _():
        share_part[...] = with_seventh(t2)

    @pl.when((core != 0) & (k == 2))
    def _():
        far_share[...] = with_seventh(far).astype(LOW)

    @pl.when((core == 0) | (k != 2))
    def _():
        far_share[...] = jnp.zeros((ROWS, D), LOW)


def own_line(
    k_ref, scale_ref, shift_ref, t0, t2, i0, i1, i2, coef0, gt0p, own_part, share_part,
    ours, share, gt0, texts, coef, pictures,
):
    k = k_ref[0]
    texts[0:ROWS] = t2[...]
    texts[ROWS:] = t0[...]
    coef[ROWS:] = coef0[...]
    pictures[0:ROWS] = i0[...]
    pictures[ROWS : 2 * ROWS] = i1[...]
    pictures[2 * ROWS :] = i2[...]
    value = negatives(t2[...], pictures[...], scale_ref, shift_ref)
    column = lax.broadcasted_iota(jnp.int32, value.shape, 1)
    unused = (column >= ROWS) & (column < 2 * ROWS) & (k == 0)
    coef[0:ROWS] = jnp.where(unused, 0.0, value).astype(LOW)
    share[...] = (share_part[...] + matmul(coef[0:ROWS], pictures[...])).astype(LOW)
    ours[...] = over_texts(coef[...], texts[...])
    gt0[...] = gt0p[...] + own_part[...]


def both_cores(ours, received, gi0, gi1, gi2):
    gi0[...] = ours[0:ROWS] + received[0:ROWS].astype(F32)
    gi1[...] = (ours[ROWS : 2 * ROWS] + received[ROWS : 2 * ROWS].astype(F32)).astype(LOW)
    gi2[...] = (ours[2 * ROWS :] + received[2 * ROWS :].astype(F32)).astype(LOW)


def kernel_call(body, n_small, args, outs, scratch=()):
    return pl.pallas_call(
        body,
        out_shape=[jax.ShapeDtypeStruct(shape, kind) for shape, kind in outs],
        in_specs=[pl.BlockSpec(memory_space=pltpu.SMEM)] * n_small
        + [pl.BlockSpec(memory_space=pltpu.VMEM)] * (len(args) - n_small),
        out_specs=[pl.BlockSpec(memory_space=pltpu.VMEM)] * len(outs),
        scratch_shapes=[pltpu.VMEM(shape, LOW) for shape in scratch],
        compiler_params=pltpu.CompilerParams(vmem_limit_bytes=12 * 1024 * 1024),
    )(*args)


def on_device(
    picture_embedding_matrix,
    caption_embedding_matrix,
    positive_caption_indices,
    sharpness_multiplier,
    additive_shift_term,
):
    here = lax.axis_index(AXES)
    k = here % LINE
    core = core_of(here)
    y = lap_of(here)
    image0, text0 = picture_embedding_matrix, caption_embedding_matrix
    small = [k.astype(jnp.int32).reshape(1), sharpness_multiplier, additive_shift_term]
    wanted = jnp.concatenate([positive_caption_indices - here * ROWS, jnp.full((2 * ROWS,), -1, jnp.int32)])[None]
    block, three = (ROWS, D), LINE * ROWS

    corner = detour(text0, 1)
    main = straight(text0, 1)
    image1 = line_turned(image0, 1)
    image2 = line_turned(image0, 2)
    far = sent(text0, lambda b: b + 2 * GROUP if b % GROUP == 5 else None)
    relayed = after_detour(corner, 1)
    others = [cores_swapped(image1), cores_swapped(jnp.stack([image0, image2]))]
    raw = image1, image2
    image1, image2, far, main, relayed = lax.optimization_barrier((image1, image2, far, main, relayed))
    coef0, gt0 = kernel_call(
        own_texts,
        3,
        small + [wanted, image0, *raw, text0],
        [((ROWS, three), LOW), (block, F32)],
        [(three, D)],
    )
    text2 = jnp.where(y == 0, relayed, main)
    coef0, far = lax.optimization_barrier((coef0, far))
    theirs, own_part, share_part, far = kernel_call(
        other_line,
        4,
        [small[0], core.astype(jnp.int32).reshape(1), *small[1:], text0, text2, far, *others],
        [((three, D), LOW), (block, F32), (block, F32), (block, LOW)],
        [(ROWS, D), (three, D)],
    )
    ours, share, gt0 = kernel_call(
        own_line,
        3,
        [*small, text0, text2, image0, image1, image2, coef0, gt0, own_part, share_part],
        [((three, D), F32), (block, LOW), (block, F32)],
        [(2 * ROWS, D), (2 * ROWS, three), (three, D)],
    )
    received = cores_swapped(theirs)
    back_corner = detour(share, -1)
    back_main = straight(share, -1)
    gi0, gi1, gi2 = kernel_call(
        both_cores, 0, [ours, received], [(block, F32), (block, LOW), (block, LOW)]
    )
    far_back = sent(far, lambda b: b - 2 * GROUP if b % GROUP == 5 else None)
    back1 = line_turned(gi1, -1)
    back2 = line_turned(gi2, -2)
    back_relayed = after_detour(back_corner, -1)
    grad_image = gi0 + (back1.astype(F32) + back2.astype(F32))
    grad_image, gt0 = lax.optimization_barrier((grad_image, gt0))
    back_text = jnp.where(y == LAP - 1, back_relayed, back_main)
    grad_text = gt0 + (back_text.astype(F32) + jnp.where(here % GROUP == 5, far_back.astype(F32), 0.0))
    return grad_image, grad_text


def solution(mesh):
    in_specs = (P(AXES, None), P(AXES, None), P(AXES), P(), P())
    out_specs = (P(AXES, None), P(AXES, None))
    return jax.shard_map(
        on_device, mesh=mesh, in_specs=in_specs, out_specs=out_specs, check_vma=False
    )
```

```python
import jax
import jax.numpy as jnp
from jax import lax
from jax.experimental import pallas as pl
from jax.experimental.pallas import tpu as pltpu
from jax.sharding import PartitionSpec as P

AXES = ("dp", "mp")
ROWS = 192
D = 1152
LINE = 3
GROUP = 6
LAP = 8
LAPS = 4
NB = 768
LOW = jnp.bfloat16
F32 = jnp.float32


def lap_of(b):
    return (b // GROUP) % LAP


def core_of(b):
    return b // LINE % 2


def sent(value, target):
    pairs = [(b, target(b) % NB) for b in range(NB) if target(b) is not None]
    return lax.ppermute(value, AXES, pairs)


def line_turned(value, by):
    return sent(value, lambda b: b // LINE * LINE + (b + by) % LINE)


def cores_swapped(value):
    return sent(value, lambda b: b + LINE if core_of(b) == 0 else b - LINE)


def plane(b, by):
    step = b % LINE if core_of(b) == 0 else GROUP - 1 - b % LINE
    return step if by > 0 else LAP - 1 - step


def at(x, lap, y, place):
    return ((x % LAPS * LAPS + lap % LAPS) * LAP + y) * GROUP + place


def detour(value, by):
    start, last = (LAP - 1, LAPS - 1) if by > 0 else (0, 0)

    def target(b):
        x, lap = b // (GROUP * LAP * LAPS), b // (GROUP * LAP) % LAPS
        return at(x + (by if lap == last else 0), lap, plane(b, by), b % GROUP) if lap_of(b) == start else None

    return sent(value, target)


def after_detour(value, by):
    end = 0 if by > 0 else LAP - 1

    def target(b):
        x, lap = b // (GROUP * LAP * LAPS), b // (GROUP * LAP) % LAPS
        return at(x, lap + by, end, b % GROUP) if lap_of(b) == plane(b, by) else None

    return sent(value, target)


def straight(value, by):
    start = LAP - 1 if by > 0 else 0
    return sent(value, lambda b: None if lap_of(b) == start else b + by * GROUP)


def scores(texts, pictures):
    return lax.dot_general(texts, pictures, (((1,), (1,)), ((), ())), preferred_element_type=F32)


def matmul(a, b):
    return jnp.dot(a, b, preferred_element_type=F32)


def own_texts(k_ref, scale_ref, shift_ref, wanted, i0, i1, i2, t0, coef, gt0, pictures):
    scale, shift, k = scale_ref[0], shift_ref[0], k_ref[0]
    pictures[0:ROWS] = i0[...]
    pictures[ROWS : 2 * ROWS] = i1[...]
    pictures[2 * ROWS :] = i2[...]
    logits = scores(t0[...], pictures[...])
    row = lax.broadcasted_iota(jnp.int32, logits.shape, 0)
    column = lax.broadcasted_iota(jnp.int32, logits.shape, 1)
    sign = jnp.where(wanted[...] == row, -1.0, 1.0).astype(F32)
    value = scale * sign * jax.nn.sigmoid(sign * (scale * logits + shift))
    one = (column >= ROWS) & (column < 2 * ROWS)
    unused = (one & (k != 0)) | ((column >= 2 * ROWS) & (k == 2))
    coef[...] = jnp.where(unused, 0.0, value).astype(LOW)
    gt0[...] = matmul(coef[...], pictures[...])


def over_texts(coef, texts):
    return lax.dot_general(coef, texts, (((0,), (0,)), ((), ())), preferred_element_type=F32)


def over_texts(coef, texts):
    return lax.dot_general(coef, texts, (((0,), (0,)), ((), ())), preferred_element_type=F32)


def negatives(texts, pictures, scale_ref, shift_ref):
    scale, shift = scale_ref[0], shift_ref[0]
    return scale * jax.nn.sigmoid(scale * scores(texts, pictures) + shift)


def other_line(
    k_ref, core_ref, scale_ref, shift_ref, t0, t2, far, o1, o02,
    theirs, own_part, share_part, far_share, spare, others,
):
    k, core = k_ref[0], core_ref[0]
    others[0:ROWS] = o02[0]
    others[ROWS : 2 * ROWS] = o1[...]
    others[2 * ROWS :] = o02[1]

    @pl.when(core == 0)
    def _():
        spare[...] = t0[...]

    @pl.when(core != 0)
    def _():
        spare[...] = t2[...]

    full = negatives(spare[...], others[...], scale_ref, shift_ref).astype(LOW)
    by_image = over_texts(full, spare[...])
    theirs[0 : 2 * ROWS] = by_image[0 : 2 * ROWS].astype(LOW)
    by_text = matmul(full, others[...])

    @pl.when(k != 2)
    def _():
        theirs[2 * ROWS :] = by_image[2 * ROWS :].astype(LOW)

    def with_seventh(text):
        single = negatives(text[...], others[2 * ROWS :], scale_ref, shift_ref).astype(LOW)
        theirs[2 * ROWS :] = (by_image[2 * ROWS :] + over_texts(single, text[...])).astype(LOW)
        return matmul(single, others[2 * ROWS :])

    @pl.when(core == 0)
    def _():
        own_part[...] = by_text

    @pl.when(core != 0)
    def _():
        own_part[...] = jnp.zeros((ROWS, D), F32)
        share_part[...] = by_text

    @pl.when((core == 0) & (k != 2))
    def _():
        share_part[...] = jnp.zeros((ROWS, D), F32)

    @pl.when((core == 0) & (k == 2))
    def _():
        share_part[...] = with_seventh(t2)

    @pl.when((core != 0) & (k == 2))
    def _():
        far_share[...] = with_seventh(far).astype(LOW)

    @pl.when((core == 0) | (k != 2))
    def _():
        far_share[...] = jnp.zeros((ROWS, D), LOW)


def own_line(
    k_ref, scale_ref, shift_ref, t0, t2, i0, i1, i2, coef0, gt0p, own_part, share_part,
    ours, share, gt0, texts, coef, pictures,
):
    k = k_ref[0]
    texts[0:ROWS] = t2[...]
    texts[ROWS:] = t0[...]
    coef[ROWS:] = coef0[...]
    pictures[0:ROWS] = i0[...]
    pictures[ROWS : 2 * ROWS] = i1[...]
    pictures[2 * ROWS :] = i2[...]
    value = negatives(t2[...], pictures[...], scale_ref, shift_ref)
    column = lax.broadcasted_iota(jnp.int32, value.shape, 1)
    unused = (column >= ROWS) & (column < 2 * ROWS) & (k == 0)
    coef[0:ROWS] = jnp.where(unused, 0.0, value).astype(LOW)
    share[...] = (share_part[...] + matmul(coef[0:ROWS], pictures[...])).astype(LOW)
    ours[...] = over_texts(coef[...], texts[...])
    gt0[...] = gt0p[...] + own_part[...]


def both_cores(ours, received, gi1, gi2):
    gi1[...] = (ours[ROWS : 2 * ROWS] + received[ROWS : 2 * ROWS].astype(F32)).astype(LOW)
    gi2[...] = (ours[2 * ROWS :] + received[2 * ROWS :].astype(F32)).astype(LOW)


def kernel_call(body, n_small, args, outs, scratch=()):
    return pl.pallas_call(
        body,
        out_shape=[jax.ShapeDtypeStruct(shape, kind) for shape, kind in outs],
        in_specs=[pl.BlockSpec(memory_space=pltpu.SMEM)] * n_small
        + [pl.BlockSpec(memory_space=pltpu.VMEM)] * (len(args) - n_small),
        out_specs=[pl.BlockSpec(memory_space=pltpu.VMEM)] * len(outs),
        scratch_shapes=[pltpu.VMEM(shape, LOW) for shape in scratch],
        compiler_params=pltpu.CompilerParams(vmem_limit_bytes=12 * 1024 * 1024),
    )(*args)


def on_device(
    picture_embedding_matrix,
    caption_embedding_matrix,
    positive_caption_indices,
    sharpness_multiplier,
    additive_shift_term,
):
    here = lax.axis_index(AXES)
    k = here % LINE
    core = core_of(here)
    y = lap_of(here)
    image0, text0 = picture_embedding_matrix, caption_embedding_matrix
    small = [k.astype(jnp.int32).reshape(1), sharpness_multiplier, additive_shift_term]
    wanted = jnp.concatenate([positive_caption_indices - here * ROWS, jnp.full((2 * ROWS,), -1, jnp.int32)])[None]
    block, three = (ROWS, D), LINE * ROWS

    corner = detour(text0, 1)
    main = straight(text0, 1)
    image1 = line_turned(image0, 1)
    image2 = line_turned(image0, 2)
    far = sent(text0, lambda b: b + 2 * GROUP if b % GROUP == 5 else None)
    relayed = after_detour(corner, 1)
    others = [cores_swapped(image1), cores_swapped(jnp.stack([image0, image2]))]
    raw = image1, image2
    image1, image2, far, main, relayed = lax.optimization_barrier((image1, image2, far, main, relayed))
    coef0, gt0 = kernel_call(
        own_texts,
        3,
        small + [wanted, image0, *raw, text0],
        [((ROWS, three), LOW), (block, F32)],
        [(three, D)],
    )
    text2 = jnp.where(y == 0, relayed, main)
    coef0, far = lax.optimization_barrier((coef0, far))
    theirs, own_part, share_part, far = kernel_call(
        other_line,
        4,
        [small[0], core.astype(jnp.int32).reshape(1), *small[1:], text0, text2, far, *others],
        [((three, D), LOW), (block, F32), (block, F32), (block, LOW)],
        [(ROWS, D), (three, D)],
    )
    ours, share, gt0 = kernel_call(
        own_line,
        3,
        [*small, text0, text2, image0, image1, image2, coef0, gt0, own_part, share_part],
        [((three, D), F32), (block, LOW), (block, F32)],
        [(2 * ROWS, D), (2 * ROWS, three), (three, D)],
    )
    received = cores_swapped(theirs)
    back_corner = detour(share, -1)
    back_main = straight(share, -1)
    gi1, gi2 = kernel_call(both_cores, 0, [ours, received], [(block, LOW), (block, LOW)])
    far_back = sent(far, lambda b: b - 2 * GROUP if b % GROUP == 5 else None)
    back1 = line_turned(gi1, -1)
    back2 = line_turned(gi2, -2)
    back_relayed = after_detour(back_corner, -1)
    gi0 = ours[:ROWS] + received[:ROWS].astype(F32)
    grad_image = gi0 + (back1.astype(F32) + back2.astype(F32))
    grad_image, gt0 = lax.optimization_barrier((grad_image, gt0))
    back_text = jnp.where(y == LAP - 1, back_relayed, back_main)
    grad_text = gt0 + (back_text.astype(F32) + jnp.where(here % GROUP == 5, far_back.astype(F32), 0.0))
    return grad_image, grad_text


def solution(mesh):
    in_specs = (P(AXES, None), P(AXES, None), P(AXES), P(), P())
    out_specs = (P(AXES, None), P(AXES, None))
    return jax.shard_map(
        on_device, mesh=mesh, in_specs=in_specs, out_specs=out_specs, check_vma=False
    )
```
